32 devices in a mesh: grp: 2 (over x), exp: 4 (over y, core), dp: 4 (over z).
Axes of the slice: x: 2, y: 2, z: 4, core: 2. Of those that a mesh axis runs over, the one named last changes fastest.
Arguments:
- tokens: bfloat16 [4096, 4096], P(('grp', 'exp', 'dp')), parts along dimension 0
- expert_ids: int32 [4096, 8], P(('grp', 'exp', 'dp')), parts along dimension 0, may hold values from 0 to 127, as said below
- router_weight: float32 [4096, 8], P(('grp', 'exp', 'dp')), parts along dimension 0, may hold values from 0.05 to 1
- window_ids: int32 [8], P('grp'), parts along dimension 0, may hold values from 0 to 127, as said below
- gate_weight: bfloat16 [8, 4096, 1536], P(('grp', 'exp'), None, 'dp'), parts along dimension 0, may hold values from -0.09375 to 0.09375
- up_weight: bfloat16 [8, 4096, 1536], P(('grp', 'exp'), None, 'dp'), parts along dimension 0, may hold values from -0.09375 to 0.09375
- down_weight: bfloat16 [8, 1536, 4096], P(('grp', 'exp'), 'dp'), parts along dimension 0, may hold values from -0.15625 to 0.15625
Outputs:
- combined: bfloat16 [4096, 4096], P(('grp', 'exp', 'dp')), parts along dimension 0
- gram_out: bfloat16 [8, 4096, 4096], P(('grp', 'exp'), None, 'dp'), parts along dimension 0
The draws below stay inside these ranges and needn't reach their ends.
There are 2 independent parts, one for each index of `grp`. The reference program is written for one: setup_inputs(seed, part) draws one part's arguments, and reference() takes and returns one part's arrays. A program takes and returns all parts, laid end to end along the dimension named above; each array names one. Nothing has to cross between parts.
Inputs may be any that keep to these rules, and one draw needn't show every extreme that they name: `expert_ids`: each row names 8 different experts; in each aligned block of 128 rows (the rows of one device) every window expert is named by 1 to 8 rows, and some window expert by exactly 8 rows in every block. `window_ids`: 4 different experts; experts 0 and 127 are always among them.
All inputs are finite; a program needn't handle non-finite values.
Results may differ from the reference program's by a relative error of at most 0.0058.
Values may be sent and summed in bfloat16 or wider, within the bound.
No kernel may reach another device: no remote copies, remote signals or barrier semaphores. Data moves between devices by JAX's collectives and lax.ppermute only.
A program may use at most 128 MiB of HBM per device.

```python
import math
import jax
import jax.numpy as jnp
from jax import lax

D = 4096
FF = 1536
EXPERTS_ALL = 128
TOPK = 8
TOK_DEV = 128
CAP = 8
WINDOW = 4
TOKENS = 2048


def place_value(ordering, value, slot):
    where_now = jnp.argmax(ordering == value).astype(jnp.int32)
    held = ordering[slot]
    ordering = ordering.at[where_now].set(held)
    return ordering.at[slot].set(value).astype(jnp.int32)


def expert_order(key):
    subkeys = jax.random.split(key, 2)
    ordering = jax.random.permutation(subkeys[0], EXPERTS_ALL).astype(jnp.int32)
    first_slot = jax.random.randint(subkeys[1], (), 0, WINDOW).astype(jnp.int32)
    second_slot = ((first_slot + 1) % WINDOW).astype(jnp.int32)
    ordering = place_value(ordering, EXPERTS_ALL - 1, first_slot)
    ordering = place_value(ordering, 0, second_slot)
    return ordering


def draw_window_ids(key, part):
    ordering = expert_order(key)
    return ordering[:WINDOW].astype(jnp.int32)


def draw_expert_ids(key, part):
    ordering = expert_order(key)
    key = jax.random.fold_in(key, 11)
    key_list = jax.random.split(key, 7)
    blocks = TOKENS // TOK_DEV
    window = ordering[:WINDOW]
    others = ordering[WINDOW:]
    spare_count = EXPERTS_ALL - WINDOW
    first_draw = jax.random.randint(key_list[0], (blocks, WINDOW), 0, CAP + 1)
    second_draw = jax.random.randint(key_list[1], (blocks, WINDOW), 0, CAP + 1)
    counts = jnp.minimum(1 + first_draw * second_draw // CAP, CAP)
    slot_index = jnp.arange(WINDOW)
    hot_part = jax.random.randint(key_list[2], (), 0, WINDOW)
    hot_block = jax.random.randint(key_list[3], (blocks, 1), 0, WINDOW)
    counts = jnp.where((slot_index[None, :] == hot_part) | (slot_index[None, :] == hot_block), CAP, counts)
    offsets = jnp.cumsum(counts, axis=1) - counts
    positions = jax.vmap(lambda subkey: jax.random.permutation(subkey, TOK_DEV))(jax.random.split(key_list[4], blocks))
    member = (positions[:, :, None] - offsets[:, None, :]) % TOK_DEV < counts[:, None, :]
    member_int = member.astype(jnp.int32)
    ranking = jnp.cumsum(member_int, axis=2) - member_int
    pick_index = jnp.arange(TOPK)
    window_pick = jnp.sum(jnp.where(member[:, :, :, None] & (ranking[:, :, :, None] == pick_index), window[None, None, :, None], 0), axis=2)
    in_window = jnp.sum(member_int, axis=2)
    starts = jax.random.randint(key_list[5], (blocks, TOK_DEV), 0, spare_count)
    other_pick = others[(starts[:, :, None] + pick_index - in_window[:, :, None]) % spare_count]
    chosen = jnp.where(pick_index < in_window[:, :, None], window_pick, other_pick)
    scores = jax.random.randint(key_list[6], (blocks, TOK_DEV, TOPK), 0, 1 << 20) * TOPK + pick_index
    shuffle = jnp.argsort(scores, axis=-1)
    chosen = jnp.take_along_axis(chosen, shuffle, axis=-1)
    return chosen.reshape(TOKENS, TOPK).astype(jnp.int32)


def draw_tokens(key, part):
    key = jax.random.fold_in(key, 5)
    key_list = jax.random.split(key, 3)
    common = jax.random.normal(key_list[0], (D,), jnp.float32)
    noise = jax.random.normal(key_list[1], (TOKENS, D), jnp.float32)
    weights = jax.random.normal(key_list[2], (TOKENS, 1), jnp.float32)
    return jnp.clip(noise + 0.8 * weights * common[None, :], -8.0, 8.0).astype(jnp.bfloat16)


def block_scale(key, extent, shards, least, largest):
    def one(position, parts):
        heights = jax.random.uniform(jax.random.fold_in(jax.random.fold_in(key, 6), position), (parts,), jnp.float32, least / len(shards), largest / len(shards))
        return jnp.repeat(jnp.exp(heights), extent[position] // parts).reshape((-1,) + (1,) * (len(extent) - position - 1))

    factor_of = one(*shards[0])
    for cut in shards[1:]:
        factor_of = factor_of * one(*cut)
    return factor_of


def gaussian(own_key, extent, deviation, limit, cuts=(), kind=jnp.bfloat16):
    level = block_scale(own_key, extent, cuts, -0.22, 0.18) if cuts else 1.0
    result = jax.random.normal(own_key, extent, jnp.float32) * deviation * level
    return jnp.minimum(jnp.maximum(result, -limit), limit).astype(kind)


def setup_inputs(seed: int = 0, part: int = 0) -> dict:
    seeds = jax.random.split(jax.random.key(seed), 8)
    part_splits = jax.random.split(jax.random.fold_in(seeds[7], part), 8)
    tokens = draw_tokens(jax.random.fold_in(jax.random.fold_in(seeds[7], part), 71), part)
    expert_ids = draw_expert_ids(jax.random.fold_in(jax.random.fold_in(seeds[7], part), 71), part)
    router_weight = jnp.clip(jnp.exp(math.log(1.0) - 2.9957323 * jax.random.uniform(part_splits[2], (TOKENS, TOPK), jnp.float32) ** block_scale(part_splits[2], (TOKENS, TOPK), ((0, 16),), -0.2, 0.2)), 0.05, 1.0)
    window_ids = draw_window_ids(jax.random.fold_in(jax.random.fold_in(seeds[7], part), 71), part)
    gate_weight = gaussian(part_splits[4], (WINDOW, D, FF), D ** -0.5, 0.09375, ((0, 4), (2, 4)))
    up_weight = gaussian(part_splits[5], (WINDOW, D, FF), D ** -0.5, 0.09375, ((0, 4), (2, 4)))
    down_weight = gaussian(part_splits[6], (WINDOW, FF, D), FF ** -0.5, 0.15625, ((0, 4), (1, 4)))
    return dict(tokens=tokens, expert_ids=expert_ids, router_weight=router_weight, window_ids=window_ids, gate_weight=gate_weight, up_weight=up_weight, down_weight=down_weight)


def reference(tokens, expert_ids, router_weight, window_ids, gate_weight, up_weight, down_weight):
    row_limit = (TOKENS // TOK_DEV) * CAP
    scaling = EXPERTS_ALL / (TOPK * TOKENS)
    positions = jnp.arange(row_limit, dtype=jnp.int32)

    def one_expert(combined, slot_index):
        matches = expert_ids == window_ids[slot_index]
        routed = jnp.any(matches, axis=1)
        shares = jnp.sum(jnp.where(matches, router_weight, 0.0), axis=1)
        picked = jnp.nonzero(routed, size=row_limit, fill_value=0)[0].astype(jnp.int32)
        validity = (positions < jnp.sum(routed.astype(jnp.int32))).astype(jnp.float32)
        chosen_rows = tokens[picked]
        gate_part = jnp.dot(chosen_rows, gate_weight[slot_index], preferred_element_type=jnp.float32)
        up_part = jnp.dot(chosen_rows, up_weight[slot_index], preferred_element_type=jnp.float32)
        hidden = (jax.nn.silu(gate_part) * up_part).astype(jnp.bfloat16)
        expert_out = (jnp.dot(hidden, down_weight[slot_index], preferred_element_type=jnp.float32) * validity[:, None]).astype(jnp.bfloat16)
        gram_sum = lax.dot_general(expert_out, expert_out, (((0,), (0,)), ((), ())), preferred_element_type=jnp.float32)
        gram_out = (gram_sum * scaling).astype(jnp.bfloat16)
        combined = combined.at[picked].add(expert_out.astype(jnp.float32) * (shares[picked] * validity)[:, None])
        return combined, gram_out

    combined, all_grams = lax.scan(one_expert, jnp.zeros((TOKENS, D), jnp.float32), jnp.arange(WINDOW, dtype=jnp.int32))
    return combined.astype(jnp.bfloat16), all_grams
```

```python
import jax
import jax.numpy as jnp
from jax import lax
from jax.sharding import PartitionSpec as P

EXPERTS_ALL = 128
TOPK = 8
CAP = 8


def swap(x, axis, k):
    n = lax.axis_size(axis)
    return lax.ppermute(x, axis, [(i, i ^ k) for i in range(n)])


def gather_blocks(own, axis):
    n = lax.axis_size(axis)
    held = {0: own}
    bit = n // 2
    while bit:
        for r in list(held):
            held[r ^ bit] = swap(held[r], axis, bit)
        bit //= 2
    return [held[r] for r in range(n)]


def reduce_blocks(blocks, axis):
    n = lax.axis_size(axis)
    held = dict(enumerate(blocks))
    bit = 1
    while bit < n:
        keep = [r for r in held if not r & bit]
        keep.sort(reverse=True)
        held = {
            r: held[r] + swap(held[r ^ bit].astype(jnp.bfloat16), axis, bit).astype(jnp.float32)
            for r in keep
        }
        bit *= 2
    return held[0]


def local(tokens, expert_ids, router_weight, window_ids, gate_weight, up_weight, down_weight):
    tok_count, feat_width = tokens.shape
    window_size = window_ids.shape[0]
    owner_count = lax.axis_size("exp")
    shard_count = lax.axis_size("dp")
    slots = lax.axis_index("exp") ^ jnp.arange(window_size, dtype=jnp.int32)
    window = jnp.sum(
        jnp.where(
            slots[:, None] == jnp.arange(window_size, dtype=jnp.int32)[None, :],
            window_ids[None, :],
            0,
        ),
        axis=1,
    )
    matches = expert_ids[:, :, None] == window[None, None, :]
    routed = jnp.any(matches, axis=1).astype(jnp.float32)
    shares = jnp.sum(jnp.where(matches, router_weight[:, :, None], 0.0), axis=1)
    slot_ids = jnp.cumsum(routed, axis=0) - routed
    slot_range = jnp.arange(CAP, dtype=jnp.float32)
    placing = (slot_ids.T[:, None, :] == slot_range[None, :, None]).astype(jnp.float32) * routed.T[
        :, None, :
    ]
    placing = placing.reshape(window_size * CAP, tok_count)
    outgoing = jnp.dot(
        placing.astype(jnp.bfloat16), tokens, preferred_element_type=jnp.float32
    ).astype(jnp.bfloat16)
    pieces = [
        swap(outgoing[k * CAP : (k + 1) * CAP], "exp", k) if k else outgoing[:CAP]
        for k in range(owner_count)
    ]
    own_rows = jnp.concatenate(pieces, axis=0)
    row_block = jnp.concatenate(gather_blocks(own_rows, "dp"), axis=0)
    gate_part = jnp.dot(row_block, gate_weight[0], preferred_element_type=jnp.float32)
    up_part = jnp.dot(row_block, up_weight[0], preferred_element_type=jnp.float32)
    hidden = (jax.nn.silu(gate_part) * up_part).astype(jnp.bfloat16)
    partial = jnp.dot(hidden, down_weight[0], preferred_element_type=jnp.float32)
    own_count = owner_count * CAP
    blocks = [partial[r * own_count : (r + 1) * own_count] for r in range(shard_count)]
    expert_out = reduce_blocks(blocks, "dp").astype(jnp.bfloat16)
    col_width = feat_width // shard_count
    col_start = lax.axis_index("dp") * col_width
    row_block = jnp.concatenate(gather_blocks(expert_out, "dp"), axis=0)
    column_block = lax.dynamic_slice_in_dim(row_block, col_start, col_width, 1)
    gram_sum = lax.dot_general(
        row_block, column_block, (((0,), (0,)), ((), ())), preferred_element_type=jnp.float32
    )
    scaling = EXPERTS_ALL / (TOPK * tok_count * owner_count * shard_count)
    gram_out = (gram_sum * scaling).astype(jnp.bfloat16)[None]
    returned = jnp.concatenate(
        [
            swap(expert_out[k * CAP : (k + 1) * CAP], "exp", k) if k else expert_out[:CAP]
            for k in range(owner_count)
        ],
        axis=0,
    )
    weighted = placing.reshape(window_size, CAP, tok_count) * shares.T[:, None, :]
    combined = lax.dot_general(
        weighted.reshape(window_size * CAP, tok_count),
        returned.astype(jnp.float32),
        (((0,), (0,)), ((), ())),
        precision=lax.Precision.HIGHEST,
        preferred_element_type=jnp.float32,
    )
    return (combined.astype(jnp.bfloat16), gram_out)


def solution(mesh):
    in_specs = (
        P(("grp", "exp", "dp"), None),
        P(("grp", "exp", "dp"), None),
        P(("grp", "exp", "dp"), None),
        P("grp"),
        P(("grp", "exp"), None, "dp"),
        P(("grp", "exp"), None, "dp"),
        P(("grp", "exp"), "dp", None),
    )
    out_specs = (P(("grp", "exp", "dp"), None), P(("grp", "exp"), None, "dp"))
    return jax.shard_map(local, mesh=mesh, in_specs=in_specs, out_specs=out_specs, check_vma=False)
```

```python
import functools

import jax
import jax.numpy as jnp
from jax import lax
from jax.experimental import pallas as pl
from jax.experimental.pallas import tpu as pltpu
from jax.sharding import PartitionSpec as P

EXPERTS_ALL = 128
TOPK = 8
CAP = 8
MIB = 1 << 20
VMEM = pl.BlockSpec(memory_space=pltpu.VMEM)
SMEM = pl.BlockSpec(memory_space=pltpu.SMEM)
HBM = pl.BlockSpec(memory_space=pltpu.HBM)


def in_hbm(x):
    return pltpu.with_memory_space_constraint(x, pltpu.HBM)


def swap(x, axis, k):
    n = lax.axis_size(axis)
    return lax.ppermute(x, axis, [(i, i ^ k) for i in range(n)])


def gather_blocks(own, axis):
    n = lax.axis_size(axis)
    held = {0: own}
    bit = n // 2
    while bit:
        for r in list(held):
            held[r ^ bit] = swap(held[r], axis, bit)
        bit //= 2
    return [held[r] for r in range(n)]


def reduce_blocks(blocks, axis):
    n = lax.axis_size(axis)
    held = dict(enumerate(blocks))
    bit = 1
    while bit < n:
        keep = [r for r in held if not r & bit]
        keep.sort(reverse=True)
        held = {
            r: held[r].astype(jnp.float32)
            + swap(held[r ^ bit].astype(jnp.bfloat16), axis, bit).astype(jnp.float32)
            for r in keep
        }
        bit *= 2
    return held[0]


def pack_kernel(count, place_ref, window_hbm, ids_hbm, weight_hbm, tokens_hbm, *refs):
    pieces, weighted_ref = refs[:count], refs[count]
    window_ref, ids_ref, weight_ref, tokens_ref, sems = refs[count + 1 :]
    tok_count, width = tokens_ref.shape
    step = 1024
    small = [
        pltpu.make_async_copy(source, target, sems.at[i])
        for i, (source, target) in enumerate(
            ((window_hbm, window_ref), (ids_hbm, ids_ref), (weight_hbm, weight_ref))
        )
    ]
    parts = [slice(start, start + step) for start in range(0, width, step)]
    large = [
        pltpu.make_async_copy(tokens_hbm.at[:, part], tokens_ref.at[:, part], sems.at[3 + i])
        for i, part in enumerate(parts)
    ]
    for copy in small + large:
        copy.start()
    for copy in small:
        copy.wait()
    ids = ids_ref[...]
    weights = weight_ref[...]
    routed, shares = [], []
    for k in range(count):
        match = ids == window_ref[place_ref[0] ^ k]
        routed.append(jnp.max(match.astype(jnp.float32), axis=0, keepdims=True))
        shares.append(jnp.sum(jnp.where(match, weights, 0.0), axis=0, keepdims=True))
    earlier = lax.broadcasted_iota(jnp.int32, (tok_count, tok_count), 0) < lax.broadcasted_iota(
        jnp.int32, (tok_count, tok_count), 1
    )
    ranks = jnp.dot(
        jnp.concatenate(routed, axis=0).astype(jnp.bfloat16),
        earlier.astype(jnp.bfloat16),
        preferred_element_type=jnp.float32,
    )
    slot = lax.broadcasted_iota(jnp.int32, (CAP, tok_count), 0).astype(jnp.float32)
    placing = [
        jnp.where(slot == ranks[k : k + 1], jnp.broadcast_to(routed[k], slot.shape), 0.0)
        for k in range(count)
    ]
    weighted = jnp.concatenate([placing[k] * shares[k] for k in range(count)], axis=0)
    high = weighted.astype(jnp.bfloat16)
    rest = weighted - high.astype(jnp.float32)
    middle = rest.astype(jnp.bfloat16)
    low = (rest - middle.astype(jnp.float32)).astype(jnp.bfloat16)
    weighted_ref[...] = jnp.concatenate([high, middle, low], axis=0)
    placed = jnp.concatenate(placing, axis=0).astype(jnp.bfloat16)
    for copy, part in zip(large, parts):
        copy.wait()
        rows = jnp.dot(
            placed, tokens_ref[:, part], preferred_element_type=jnp.float32
        ).astype(jnp.bfloat16)
        for k in range(count):
            pieces[k][:, part] = rows[k * CAP : (k + 1) * CAP]


def pack(place, window_ids, expert_ids, router_weight, tokens):
    count = window_ids.shape[0]
    tok_count, width = tokens.shape
    outs = pl.pallas_call(
        functools.partial(pack_kernel, count),
        out_shape=[jax.ShapeDtypeStruct((CAP, width), jnp.bfloat16)] * count
        + [jax.ShapeDtypeStruct((3 * count * CAP, tok_count), jnp.bfloat16)],
        in_specs=[SMEM] + [HBM] * 4,
        out_specs=[VMEM] * (count + 1),
        scratch_shapes=[
            pltpu.SMEM(window_ids.shape, window_ids.dtype),
            pltpu.VMEM(expert_ids.shape[::-1], expert_ids.dtype),
            pltpu.VMEM(router_weight.shape[::-1], router_weight.dtype),
            pltpu.VMEM(tokens.shape, tokens.dtype),
            pltpu.SemaphoreType.DMA((3 + width // 1024,)),
        ],
        compiler_params=pltpu.CompilerParams(vmem_limit_bytes=8 * MIB),
        cost_estimate=pl.CostEstimate(
            flops=2 * count * CAP * tok_count * width,
            bytes_accessed=2 * tok_count * width * 2,
            transcendentals=0,
        ),
    )(place, *[in_hbm(x) for x in (window_ids, expert_ids.T, router_weight.T, tokens)])
    return outs[:count], outs[count]


def load_kernel(count, *refs):
    sources, targets, sems = refs[:count], refs[-count - 1 : -1], refs[-1]
    copies = [
        pltpu.make_async_copy(source, target, sems.at[i])
        for i, (source, target) in enumerate(zip(sources, targets))
    ]
    for copy in copies:
        copy.start()
    for copy in copies:
        copy.wait()


def load(arrays, after):
    count = len(arrays)
    return pl.pallas_call(
        functools.partial(load_kernel, count),
        out_shape=[jax.ShapeDtypeStruct(x.shape, x.dtype) for x in arrays],
        in_specs=[HBM] * count + [pl.BlockSpec(memory_space=pl.ANY)],
        out_specs=[VMEM] * count,
        scratch_shapes=[pltpu.SemaphoreType.DMA((count,))],
        compiler_params=pltpu.CompilerParams(vmem_limit_bytes=16 * MIB),
        cost_estimate=pl.CostEstimate(
            flops=0,
            bytes_accessed=sum(2 * x.size * x.dtype.itemsize for x in arrays),
            transcendentals=0,
        ),
    )(*[in_hbm(x) for x in arrays], after)


def expert_kernel(count, *refs):
    rows = refs[:count]
    gate_ref, up_ref, down_ref = refs[count : count + 3]
    outs = refs[-count:]
    width = gate_ref.shape[1]
    own = rows[0].shape[0]
    step = 1024
    gate = up = 0.0
    for start in range(0, width, step):
        part = slice(start, start + step)
        x = jnp.concatenate([r[:, part] for r in rows], axis=0)
        gate += jnp.dot(x, gate_ref[0, part, :], preferred_element_type=jnp.float32)
        up += jnp.dot(x, up_ref[0, part, :], preferred_element_type=jnp.float32)
    hidden = (gate / (1.0 + jnp.exp(-gate)) * up).astype(jnp.bfloat16)
    for start in range(0, width, step):
        part = slice(start, start + step)
        y = jnp.dot(hidden, down_ref[0, :, part], preferred_element_type=jnp.float32)
        for r in range(count):
            outs[r][:, part] = y[r * own : (r + 1) * own].astype(outs[r].dtype)


def expert(rows, gate_weight, up_weight, down_weight, after):
    count = len(rows)
    own, width = rows[0].shape
    hidden = gate_weight.shape[2]
    extra = [] if after is None else [after]
    return pl.pallas_call(
        functools.partial(expert_kernel, count),
        out_shape=[
            jax.ShapeDtypeStruct((own, width), jnp.bfloat16 if r & 1 else jnp.float32)
            for r in range(count)
        ],
        in_specs=[VMEM] * (count + 3) + [pl.BlockSpec(memory_space=pl.ANY)] * len(extra),
        out_specs=[VMEM] * count,
        compiler_params=pltpu.CompilerParams(vmem_limit_bytes=24 * MIB),
        cost_estimate=pl.CostEstimate(
            flops=4 * count * own * width * hidden * 3,
            bytes_accessed=3 * width * hidden * 2 + count * own * width * 6,
            transcendentals=count * own * hidden,
        ),
    )(*rows, gate_weight, up_weight, down_weight, *extra)


def combine_kernel(count, *refs):
    rows, weighted_ref, out_ref = refs[:count], refs[count], refs[count + 1]
    weighted = weighted_ref[...]
    width = out_ref.shape[1]
    step = 1024
    for start in range(0, width, step):
        part = slice(start, start + step)
        x = jnp.concatenate([r[:, part] for r in rows], axis=0)
        out_ref[:, part] = lax.dot_general(
            weighted,
            jnp.concatenate([x, x, x], axis=0),
            (((0,), (0,)), ((), ())),
            preferred_element_type=jnp.float32,
        ).astype(out_ref.dtype)


def combine(rows, weighted):
    count = len(rows)
    width = rows[0].shape[1]
    tok_count = weighted.shape[1]
    return pl.pallas_call(
        functools.partial(combine_kernel, count),
        out_shape=jax.ShapeDtypeStruct((tok_count, width), jnp.bfloat16),
        in_specs=[VMEM] * (count + 1),
        out_specs=VMEM,
        compiler_params=pltpu.CompilerParams(vmem_limit_bytes=8 * MIB),
        cost_estimate=pl.CostEstimate(
            flops=2 * weighted.shape[0] * tok_count * width,
            bytes_accessed=2 * tok_count * width * 2,
            transcendentals=0,
        ),
    )(*rows, weighted)


def gram_kernel(count, scaling, place_ref, *refs):
    blocks, out_ref, all_ref, own_ref = refs[:count], refs[count], refs[count + 1], refs[count + 2]
    own = blocks[0].shape[0]
    step = pl.program_id(0)

    @pl.when(step == 0)
    def _():
        for r in range(count):
            all_ref[r * own : (r + 1) * own, :] = blocks[r][...]
        width = own_ref.shape[1]
        own_ref[...] = all_ref[:, pl.ds(pl.multiple_of(place_ref[0] * width, width), width)]

    height = out_ref.shape[1]
    left = all_ref[:, pl.ds(pl.multiple_of(step * height, height), height)]
    out_ref[0] = (
        lax.dot_general(
            left, own_ref[...], (((0,), (0,)), ((), ())), preferred_element_type=jnp.float32
        )
        * scaling
    ).astype(out_ref.dtype)


def gram(place, blocks, col_width, scaling):
    count = len(blocks)
    own, width = blocks[0].shape
    height = 512
    return pl.pallas_call(
        functools.partial(gram_kernel, count, scaling),
        out_shape=jax.ShapeDtypeStruct((1, width, col_width), jnp.bfloat16),
        grid=(width // height,),
        in_specs=[SMEM] + [VMEM] * count,
        out_specs=pl.BlockSpec((1, height, col_width), lambda i: (0, i, 0)),
        scratch_shapes=[
            pltpu.VMEM((count * own, width), jnp.bfloat16),
            pltpu.VMEM((count * own, col_width), jnp.bfloat16),
        ],
        compiler_params=pltpu.CompilerParams(vmem_limit_bytes=32 * MIB),
        cost_estimate=pl.CostEstimate(
            flops=2 * count * own * width * col_width,
            bytes_accessed=width * col_width * 2 + 2 * count * own * width,
            transcendentals=0,
        ),
    )(place, *blocks)


def local(tokens, expert_ids, router_weight, window_ids, gate_weight, up_weight, down_weight):
    tok_count, feat_width = tokens.shape
    owner_count = lax.axis_size("exp")
    shard_count = lax.axis_size("dp")
    exp_place = lax.axis_index("exp").astype(jnp.int32)[None]
    dp_place = lax.axis_index("dp").astype(jnp.int32)[None]
    pieces, weighted = pack(exp_place, window_ids, expert_ids, router_weight, tokens)
    half = owner_count // 2
    gate_weight, up_weight, down_weight = load(
        (gate_weight, up_weight, down_weight), weighted
    )
    pieces = [swap(piece, "exp", k) if k else piece for k, piece in enumerate(pieces)]
    returned = []
    gram_rows = []
    after = None
    for start in range(0, owner_count, half):
        own_rows = jnp.concatenate(pieces[start : start + half], axis=0)
        rows = gather_blocks(own_rows, "dp")
        terms = expert(rows, gate_weight, up_weight, down_weight, after)
        after = terms[0]
        expert_out = reduce_blocks(terms, "dp").astype(jnp.bfloat16)
        gram_rows += gather_blocks(expert_out, "dp")
        for k in range(half):
            piece = expert_out[k * CAP : (k + 1) * CAP]
            returned.append(swap(piece, "exp", start + k) if start + k else piece)
    scaling = EXPERTS_ALL / (TOPK * tok_count * owner_count * shard_count)
    gram_out = gram(dp_place, gram_rows, feat_width // shard_count, scaling)
    combined = combine(returned, weighted)
    return (combined, gram_out)


def solution(mesh):
    in_specs = (
        P(("grp", "exp", "dp"), None),
        P(("grp", "exp", "dp"), None),
        P(("grp", "exp", "dp"), None),
        P("grp"),
        P(("grp", "exp"), None, "dp"),
        P(("grp", "exp"), None, "dp"),
        P(("grp", "exp"), "dp", None),
    )
    out_specs = (P(("grp", "exp", "dp"), None), P(("grp", "exp"), None, "dp"))
    return jax.shard_map(local, mesh=mesh, in_specs=in_specs, out_specs=out_specs, check_vma=False)
```

```python
import functools

import jax
import jax.numpy as jnp
from jax import lax
from jax.experimental import pallas as pl
from jax.experimental.pallas import tpu as pltpu
from jax.sharding import PartitionSpec as P

EXPERTS_ALL = 128
TOPK = 8
CAP = 8
MIB = 1 << 20
VMEM = pl.BlockSpec(memory_space=pltpu.VMEM)
SMEM = pl.BlockSpec(memory_space=pltpu.SMEM)
HBM = pl.BlockSpec(memory_space=pltpu.HBM)


def in_hbm(x):
    return pltpu.with_memory_space_constraint(x, pltpu.HBM)


def swap(x, axis, k):
    n = lax.axis_size(axis)
    return lax.ppermute(x, axis, [(i, i ^ k) for i in range(n)])


def after(x, *others):
    return lax.optimization_barrier((x, *others))[0] if others else x


def bits_of(axis):
    n = lax.axis_size(axis)
    return [1 << i for i in range(n.bit_length() - 1)]


def reduce_blocks(blocks, axis):
    held = dict(enumerate(blocks))
    for bit in bits_of(axis):
        keep = [r for r in held if not r & bit]
        keep.sort(reverse=True)
        arrived = {}
        for r in keep:
            term = held[r ^ bit].astype(jnp.bfloat16)
            gates = [arrived[keep[-2]]] if r == 0 and len(keep) > 1 else []
            arrived[r] = swap(after(term, *gates), axis, bit)
        held = {r: held[r].astype(jnp.float32) + arrived[r].astype(jnp.float32) for r in keep}
    return held[0]


def pack_kernel(count, place_ref, window_hbm, ids_hbm, weight_hbm, tokens_hbm, *refs):
    pieces, weighted_ref = refs[:count], refs[count]
    window_ref, ids_ref, weight_ref, tokens_ref, sems = refs[count + 1 :]
    tok_count, width = tokens_ref.shape
    step = 1024
    small = [
        pltpu.make_async_copy(source, target, sems.at[i])
        for i, (source, target) in enumerate(
            ((window_hbm, window_ref), (ids_hbm, ids_ref), (weight_hbm, weight_ref))
        )
    ]
    parts = [slice(start, start + step) for start in range(0, width, step)]
    large = [
        pltpu.make_async_copy(tokens_hbm.at[:, part], tokens_ref.at[:, part], sems.at[3 + i])
        for i, part in enumerate(parts)
    ]
    for copy in small + large:
        copy.start()
    for copy in small:
        copy.wait()
    ids = ids_ref[...]
    weights = weight_ref[...]
    routed, shares = [], []
    for k in range(count):
        match = ids == window_ref[place_ref[0] ^ k]
        routed.append(jnp.max(match.astype(jnp.float32), axis=0, keepdims=True))
        shares.append(jnp.sum(jnp.where(match, weights, 0.0), axis=0, keepdims=True))
    earlier = lax.broadcasted_iota(jnp.int32, (tok_count, tok_count), 0) < lax.broadcasted_iota(
        jnp.int32, (tok_count, tok_count), 1
    )
    ranks = jnp.dot(
        jnp.concatenate(routed, axis=0).astype(jnp.bfloat16),
        earlier.astype(jnp.bfloat16),
        preferred_element_type=jnp.float32,
    )
    slot = lax.broadcasted_iota(jnp.int32, (CAP, tok_count), 0).astype(jnp.float32)
    placing = [
        jnp.where(slot == ranks[k : k + 1], jnp.broadcast_to(routed[k], slot.shape), 0.0)
        for k in range(count)
    ]
    weighted = jnp.concatenate([placing[k] * shares[k] for k in range(count)], axis=0)
    high = weighted.astype(jnp.bfloat16)
    rest = weighted - high.astype(jnp.float32)
    middle = rest.astype(jnp.bfloat16)
    low = (rest - middle.astype(jnp.float32)).astype(jnp.bfloat16)
    weighted_ref[...] = jnp.concatenate([high, middle, low], axis=0)
    placed = jnp.concatenate(placing, axis=0).astype(jnp.bfloat16)
    for copy, part in zip(large, parts):
        copy.wait()
        rows = jnp.dot(
            placed, tokens_ref[:, part], preferred_element_type=jnp.float32
        ).astype(jnp.bfloat16)
        for k in range(count):
            pieces[k][:, part] = rows[k * CAP : (k + 1) * CAP]


def pack(place, window_ids, expert_ids, router_weight, tokens):
    count = window_ids.shape[0]
    tok_count, width = tokens.shape
    outs = pl.pallas_call(
        functools.partial(pack_kernel, count),
        out_shape=[jax.ShapeDtypeStruct((CAP, width), jnp.bfloat16)] * count
        + [jax.ShapeDtypeStruct((3 * count * CAP, tok_count), jnp.bfloat16)],
        in_specs=[SMEM] + [HBM] * 4,
        out_specs=[VMEM] * (count + 1),
        scratch_shapes=[
            pltpu.SMEM(window_ids.shape, window_ids.dtype),
            pltpu.VMEM(expert_ids.shape[::-1], expert_ids.dtype),
            pltpu.VMEM(router_weight.shape[::-1], router_weight.dtype),
            pltpu.VMEM(tokens.shape, tokens.dtype),
            pltpu.SemaphoreType.DMA((3 + width // 1024,)),
        ],
        compiler_params=pltpu.CompilerParams(vmem_limit_bytes=8 * MIB),
        cost_estimate=pl.CostEstimate(
            flops=2 * count * CAP * tok_count * width,
            bytes_accessed=2 * tok_count * width * 2,
            transcendentals=0,
        ),
    )(place, *[in_hbm(x) for x in (window_ids, expert_ids.T, router_weight.T, tokens)])
    return outs[:count], outs[count]


def load_kernel(count, *refs):
    sources, targets, sems = refs[:count], refs[-count - 1 : -1], refs[-1]
    copies = [
        pltpu.make_async_copy(source, target, sems.at[i])
        for i, (source, target) in enumerate(zip(sources, targets))
    ]
    for copy in copies:
        copy.start()
    for copy in copies:
        copy.wait()


def load(arrays, after):
    count = len(arrays)
    return pl.pallas_call(
        functools.partial(load_kernel, count),
        out_shape=[jax.ShapeDtypeStruct(x.shape, x.dtype) for x in arrays],
        in_specs=[HBM] * count + [pl.BlockSpec(memory_space=pl.ANY)],
        out_specs=[VMEM] * count,
        scratch_shapes=[pltpu.SemaphoreType.DMA((count,))],
        compiler_params=pltpu.CompilerParams(vmem_limit_bytes=16 * MIB),
        cost_estimate=pl.CostEstimate(
            flops=0,
            bytes_accessed=sum(2 * x.size * x.dtype.itemsize for x in arrays),
            transcendentals=0,
        ),
    )(*[in_hbm(x) for x in arrays], after)


def expert_kernel(count, *refs):
    rows = refs[:count]
    gate_ref, up_ref, down_ref = refs[count : count + 3]
    outs = refs[-count:]
    width = gate_ref.shape[1]
    own = rows[0].shape[0]
    step = 1024
    gate = up = 0.0
    for start in range(0, width, step):
        part = slice(start, start + step)
        x = jnp.concatenate([r[:, part] for r in rows], axis=0)
        gate += jnp.dot(x, gate_ref[0, part, :], preferred_element_type=jnp.float32)
        up += jnp.dot(x, up_ref[0, part, :], preferred_element_type=jnp.float32)
    hidden = (gate / (1.0 + jnp.exp(-gate)) * up).astype(jnp.bfloat16)
    for start in range(0, width, step):
        part = slice(start, start + step)
        y = jnp.dot(hidden, down_ref[0, :, part], preferred_element_type=jnp.float32)
        for r in range(count):
            outs[r][:, part] = y[r * own : (r + 1) * own].astype(outs[r].dtype)


def expert(rows, gate_weight, up_weight, down_weight, after):
    count = len(rows)
    own, width = rows[0].shape
    hidden = gate_weight.shape[2]
    extra = [] if after is None else [after]
    return pl.pallas_call(
        functools.partial(expert_kernel, count),
        out_shape=[
            jax.ShapeDtypeStruct((own, width), jnp.bfloat16 if r & 1 else jnp.float32)
            for r in range(count)
        ],
        in_specs=[VMEM] * (count + 3) + [pl.BlockSpec(memory_space=pl.ANY)] * len(extra),
        out_specs=[VMEM] * count,
        compiler_params=pltpu.CompilerParams(vmem_limit_bytes=24 * MIB),
        cost_estimate=pl.CostEstimate(
            flops=4 * count * own * width * hidden * 3,
            bytes_accessed=3 * width * hidden * 2 + count * own * width * 6,
            transcendentals=count * own * hidden,
        ),
    )(*rows, gate_weight, up_weight, down_weight, *extra)


def combine_kernel(count, *refs):
    rows, weighted_ref, out_ref = refs[:count], refs[count], refs[count + 1]
    weighted = weighted_ref[...]
    width = out_ref.shape[1]
    step = 1024
    for start in range(0, width, step):
        part = slice(start, start + step)
        x = jnp.concatenate([r[:, part] for r in rows], axis=0)
        out_ref[:, part] = lax.dot_general(
            weighted,
            jnp.concatenate([x, x, x], axis=0),
            (((0,), (0,)), ((), ())),
            preferred_element_type=jnp.float32,
        ).astype(out_ref.dtype)


def combine(rows, weighted):
    count = len(rows)
    width = rows[0].shape[1]
    tok_count = weighted.shape[1]
    return pl.pallas_call(
        functools.partial(combine_kernel, count),
        out_shape=jax.ShapeDtypeStruct((tok_count, width), jnp.bfloat16),
        in_specs=[VMEM] * (count + 1),
        out_specs=VMEM,
        compiler_params=pltpu.CompilerParams(vmem_limit_bytes=8 * MIB),
        cost_estimate=pl.CostEstimate(
            flops=2 * weighted.shape[0] * tok_count * width,
            bytes_accessed=2 * tok_count * width * 2,
            transcendentals=0,
        ),
    )(*rows, weighted)


def gram_kernel(count, scaling, place_ref, *refs):
    blocks = refs[:count]
    out_hbm, all_ref, own_ref, buffer, sems = refs[count:]
    own = blocks[0].shape[0]
    for r in range(count):
        all_ref[r * own : (r + 1) * own, :] = blocks[r][...]
    width = own_ref.shape[1]
    own_ref[...] = all_ref[:, pl.ds(pl.multiple_of(place_ref[0] * width, width), width)]
    steps, height = buffer.shape[:2]
    copies = []
    for i in range(steps):
        part = slice(i * height, (i + 1) * height)
        product = lax.dot_general(
            all_ref[:, part],
            own_ref[...],
            (((0,), (0,)), ((), ())),
            preferred_element_type=jnp.float32,
        )
        buffer[i] = (product * scaling).astype(buffer.dtype)
        copies.append(pltpu.make_async_copy(buffer.at[i], out_hbm.at[0, part, :], sems.at[i]))
        copies[-1].start()
    for copy in copies:
        copy.wait()


def gram(place, blocks, col_width, scaling):
    count = len(blocks)
    own, width = blocks[0].shape
    height = 256
    steps = width // height
    return pl.pallas_call(
        functools.partial(gram_kernel, count, scaling),
        out_shape=jax.ShapeDtypeStruct((1, width, col_width), jnp.bfloat16),
        in_specs=[SMEM] + [VMEM] * count,
        out_specs=HBM,
        scratch_shapes=[
            pltpu.VMEM((count * own, width), jnp.bfloat16),
            pltpu.VMEM((count * own, col_width), jnp.bfloat16),
            pltpu.VMEM((steps, height, col_width), jnp.bfloat16),
            pltpu.SemaphoreType.DMA((steps,)),
        ],
        compiler_params=pltpu.CompilerParams(vmem_limit_bytes=32 * MIB),
        cost_estimate=pl.CostEstimate(
            flops=2 * count * own * width * col_width,
            bytes_accessed=width * col_width * 2 + 2 * count * own * width,
            transcendentals=0,
        ),
    )(place, *blocks)


def local(tokens, expert_ids, router_weight, window_ids, gate_weight, up_weight, down_weight):
    tok_count, feat_width = tokens.shape
    owner_count = lax.axis_size("exp")
    shard_count = lax.axis_size("dp")
    exp_place = lax.axis_index("exp").astype(jnp.int32)[None]
    dp_place = lax.axis_index("dp").astype(jnp.int32)[None]
    pieces, weighted = pack(exp_place, window_ids, expert_ids, router_weight, tokens)
    half = owner_count // 2
    pieces = [swap(piece, "exp", k) if k else piece for k, piece in enumerate(pieces)]
    bits = bits_of("dp")
    own = [jnp.concatenate(pieces[:half], axis=0), jnp.concatenate(pieces[half:], axis=0)]

    weights = load((gate_weight, up_weight, down_weight), own[1])

    def first(own, gates):
        held = {0: own}
        for bit in reversed(bits):
            held[bit] = swap(after(own, *gates.get(bit, ())), "dp", bit)
        return held

    def later(held):
        for r in range(shard_count):
            if r not in held:
                low = r & -r
                held[r] = swap(held[r ^ low], "dp", low)
        return [held[r] for r in range(shard_count)]

    a = first(own[0], {})
    b = first(own[1], {bits[-1]: [a[bit] for bit in bits], bits[0]: [a[bit] for bit in bits]})
    a[bits[-1]] = after(a[bits[-1]], weights[0])
    rows_a = later(a)
    terms_a = expert(rows_a, *weights, None)
    rows_b = later(b)
    terms_b = expert(rows_b, *weights, terms_a[0])
    out_a = reduce_blocks(terms_a, "dp").astype(jnp.bfloat16)
    a = first(out_a, {})
    out_b = reduce_blocks(terms_b, "dp").astype(jnp.bfloat16)
    out_b = after(out_b, *[a[bit] for bit in bits])
    rows_a = later(a)
    b = first(out_b, {})
    returned = []
    for k in range(owner_count):
        source = (out_a, out_b)[k // half]
        piece = source[(k % half) * CAP : (k % half + 1) * CAP]
        returned.append(swap(piece, "exp", k) if k else piece)
    b[bits[-1]] = after(b[bits[-1]], *returned[half:])
    rows_b = later(b)
    gram_rows = rows_a + rows_b
    scaling = EXPERTS_ALL / (TOPK * tok_count * owner_count * shard_count)
    gram_out = gram(dp_place, gram_rows, feat_width // shard_count, scaling)
    combined = combine(returned, weighted)
    return (combined, gram_out)


def solution(mesh):
    in_specs = (
        P(("grp", "exp", "dp"), None),
        P(("grp", "exp", "dp"), None),
        P(("grp", "exp", "dp"), None),
        P("grp"),
        P(("grp", "exp"), None, "dp"),
        P(("grp", "exp"), None, "dp"),
        P(("grp", "exp"), "dp", None),
    )
    out_specs = (P(("grp", "exp", "dp"), None), P(("grp", "exp"), None, "dp"))
    return jax.shard_map(local, mesh=mesh, in_specs=in_specs, out_specs=out_specs, check_vma=False)
```

```python
import functools

import jax
import jax.numpy as jnp
from jax import lax
from jax.experimental import pallas as pl
from jax.experimental.pallas import tpu as pltpu
from jax.sharding import PartitionSpec as P

EXPERTS_ALL = 128
TOPK = 8
CAP = 8
MIB = 1 << 20
VMEM = pl.BlockSpec(memory_space=pltpu.VMEM)
SMEM = pl.BlockSpec(memory_space=pltpu.SMEM)
HBM = pl.BlockSpec(memory_space=pltpu.HBM)


def in_hbm(x):
    return pltpu.with_memory_space_constraint(x, pltpu.HBM)


def swap(x, axis, k):
    n = lax.axis_size(axis)
    return lax.ppermute(x, axis, [(i, i ^ k) for i in range(n)])


def after(x, *others):
    return lax.optimization_barrier((x, *others))[0] if others else x


def bits_of(axis):
    n = lax.axis_size(axis)
    return [1 << i for i in range(n.bit_length() - 1)]


def reduce_blocks(blocks, axis):
    held = dict(enumerate(blocks))
    for bit in bits_of(axis):
        keep = [r for r in held if not r & bit]
        keep.sort(reverse=True)
        held = {
            r: held[r].astype(jnp.float32)
            + swap(held[r ^ bit].astype(jnp.bfloat16), axis, bit).astype(jnp.float32)
            for r in keep
        }
    return held[0]


def pack_kernel(count, place_ref, window_hbm, ids_hbm, weight_hbm, tokens_hbm, *refs):
    pieces, weighted_ref = refs[:count], refs[count]
    window_ref, ids_ref, weight_ref, tokens_ref, sems = refs[count + 1 :]
    tok_count, width = tokens_ref.shape
    step = 1024
    small = [
        pltpu.make_async_copy(source, target, sems.at[i])
        for i, (source, target) in enumerate(
            ((window_hbm, window_ref), (ids_hbm, ids_ref), (weight_hbm, weight_ref))
        )
    ]
    parts = [slice(start, start + step) for start in range(0, width, step)]
    large = [
        pltpu.make_async_copy(tokens_hbm.at[:, part], tokens_ref.at[:, part], sems.at[3 + i])
        for i, part in enumerate(parts)
    ]
    for copy in small + large:
        copy.start()
    for copy in small:
        copy.wait()
    ids = ids_ref[...]
    weights = weight_ref[...]
    routed, shares = [], []
    for k in range(count):
        match = ids == window_ref[place_ref[0] ^ k]
        routed.append(jnp.max(match.astype(jnp.float32), axis=0, keepdims=True))
        shares.append(jnp.sum(jnp.where(match, weights, 0.0), axis=0, keepdims=True))
    earlier = lax.broadcasted_iota(jnp.int32, (tok_count, tok_count), 0) < lax.broadcasted_iota(
        jnp.int32, (tok_count, tok_count), 1
    )
    ranks = jnp.dot(
        jnp.concatenate(routed, axis=0).astype(jnp.bfloat16),
        earlier.astype(jnp.bfloat16),
        preferred_element_type=jnp.float32,
    )
    slot = lax.broadcasted_iota(jnp.int32, (CAP, tok_count), 0).astype(jnp.float32)
    placing = [
        jnp.where(slot == ranks[k : k + 1], jnp.broadcast_to(routed[k], slot.shape), 0.0)
        for k in range(count)
    ]
    weighted = jnp.concatenate([placing[k] * shares[k] for k in range(count)], axis=0)
    high = weighted.astype(jnp.bfloat16)
    rest = weighted - high.astype(jnp.float32)
    middle = rest.astype(jnp.bfloat16)
    low = (rest - middle.astype(jnp.float32)).astype(jnp.bfloat16)
    weighted_ref[...] = jnp.concatenate([high, middle, low], axis=0)
    placed = jnp.concatenate(placing, axis=0).astype(jnp.bfloat16)
    for copy, part in zip(large, parts):
        copy.wait()
        rows = jnp.dot(
            placed, tokens_ref[:, part], preferred_element_type=jnp.float32
        ).astype(jnp.bfloat16)
        for k in range(count):
            pieces[k][:, part] = rows[k * CAP : (k + 1) * CAP]


def pack(place, window_ids, expert_ids, router_weight, tokens):
    count = window_ids.shape[0]
    tok_count, width = tokens.shape
    outs = pl.pallas_call(
        functools.partial(pack_kernel, count),
        out_shape=[jax.ShapeDtypeStruct((CAP, width), jnp.bfloat16)] * count
        + [jax.ShapeDtypeStruct((3 * count * CAP, tok_count), jnp.bfloat16)],
        in_specs=[SMEM] + [HBM] * 4,
        out_specs=[VMEM] * (count + 1),
        scratch_shapes=[
            pltpu.SMEM(window_ids.shape, window_ids.dtype),
            pltpu.VMEM(expert_ids.shape[::-1], expert_ids.dtype),
            pltpu.VMEM(router_weight.shape[::-1], router_weight.dtype),
            pltpu.VMEM(tokens.shape, tokens.dtype),
            pltpu.SemaphoreType.DMA((3 + width // 1024,)),
        ],
        compiler_params=pltpu.CompilerParams(vmem_limit_bytes=8 * MIB),
        cost_estimate=pl.CostEstimate(
            flops=2 * count * CAP * tok_count * width,
            bytes_accessed=2 * tok_count * width * 2,
            transcendentals=0,
        ),
    )(place, *[in_hbm(x) for x in (window_ids, expert_ids.T, router_weight.T, tokens)])
    return outs[:count], outs[count]


def load_kernel(count, *refs):
    sources, targets, sems = refs[:count], refs[-count - 1 : -1], refs[-1]
    copies = [
        pltpu.make_async_copy(source, target, sems.at[i])
        for i, (source, target) in enumerate(zip(sources, targets))
    ]
    for copy in copies:
        copy.start()
    for copy in copies:
        copy.wait()


def load(arrays, after):
    count = len(arrays)
    return pl.pallas_call(
        functools.partial(load_kernel, count),
        out_shape=[jax.ShapeDtypeStruct(x.shape, x.dtype) for x in arrays],
        in_specs=[HBM] * count + [pl.BlockSpec(memory_space=pl.ANY)],
        out_specs=[VMEM] * count,
        scratch_shapes=[pltpu.SemaphoreType.DMA((count,))],
        compiler_params=pltpu.CompilerParams(vmem_limit_bytes=16 * MIB),
        cost_estimate=pl.CostEstimate(
            flops=0,
            bytes_accessed=sum(2 * x.size * x.dtype.itemsize for x in arrays),
            transcendentals=0,
        ),
    )(*[in_hbm(x) for x in arrays], after)


def expert_kernel(count, *refs):
    rows = refs[:count]
    gate_ref, up_ref, down_ref = refs[count : count + 3]
    outs = refs[-count:]
    width = gate_ref.shape[1]
    own = rows[0].shape[0]
    step = 1024
    gate = up = 0.0
    for start in range(0, width, step):
        part = slice(start, start + step)
        x = jnp.concatenate([r[:, part] for r in rows], axis=0)
        gate += jnp.dot(x, gate_ref[0, part, :], preferred_element_type=jnp.float32)
        up += jnp.dot(x, up_ref[0, part, :], preferred_element_type=jnp.float32)
    hidden = (gate / (1.0 + jnp.exp(-gate)) * up).astype(jnp.bfloat16)
    for start in range(0, width, step):
        part = slice(start, start + step)
        y = jnp.dot(hidden, down_ref[0, :, part], preferred_element_type=jnp.float32)
        for r in range(count):
            outs[r][:, part] = y[r * own : (r + 1) * own].astype(outs[r].dtype)


def expert(rows, gate_weight, up_weight, down_weight, after):
    count = len(rows)
    own, width = rows[0].shape
    hidden = gate_weight.shape[2]
    extra = [] if after is None else [after]
    return pl.pallas_call(
        functools.partial(expert_kernel, count),
        out_shape=[
            jax.ShapeDtypeStruct((own, width), jnp.bfloat16 if r & 1 else jnp.float32)
            for r in range(count)
        ],
        in_specs=[VMEM] * (count + 3) + [pl.BlockSpec(memory_space=pl.ANY)] * len(extra),
        out_specs=[VMEM] * count,
        compiler_params=pltpu.CompilerParams(vmem_limit_bytes=24 * MIB),
        cost_estimate=pl.CostEstimate(
            flops=4 * count * own * width * hidden * 3,
            bytes_accessed=3 * width * hidden * 2 + count * own * width * 6,
            transcendentals=count * own * hidden,
        ),
    )(*rows, gate_weight, up_weight, down_weight, *extra)


def combine_kernel(count, *refs):
    rows, weighted_ref, out_ref = refs[:count], refs[count], refs[count + 1]
    weighted = weighted_ref[...]
    width = out_ref.shape[1]
    step = 1024
    for start in range(0, width, step):
        part = slice(start, start + step)
        x = jnp.concatenate([r[:, part] for r in rows], axis=0)
        out_ref[:, part] = lax.dot_general(
            weighted,
            jnp.concatenate([x, x, x], axis=0),
            (((0,), (0,)), ((), ())),
            preferred_element_type=jnp.float32,
        ).astype(out_ref.dtype)


def combine(rows, weighted):
    count = len(rows)
    width = rows[0].shape[1]
    tok_count = weighted.shape[1]
    return pl.pallas_call(
        functools.partial(combine_kernel, count),
        out_shape=jax.ShapeDtypeStruct((tok_count, width), jnp.bfloat16),
        in_specs=[VMEM] * (count + 1),
        out_specs=VMEM,
        compiler_params=pltpu.CompilerParams(vmem_limit_bytes=8 * MIB),
        cost_estimate=pl.CostEstimate(
            flops=2 * weighted.shape[0] * tok_count * width,
            bytes_accessed=2 * tok_count * width * 2,
            transcendentals=0,
        ),
    )(*rows, weighted)


def gram_kernel(count, scaling, place_ref, *refs):
    blocks = refs[:count]
    out_hbm, all_ref, own_ref, buffer, sems = refs[count:]
    own = blocks[0].shape[0]
    for r in range(count):
        all_ref[r * own : (r + 1) * own, :] = blocks[r][...]
    width = own_ref.shape[1]
    own_ref[...] = all_ref[:, pl.ds(pl.multiple_of(place_ref[0] * width, width), width)]
    steps, height = buffer.shape[:2]
    copies = []
    for i in range(steps):
        part = slice(i * height, (i + 1) * height)
        product = lax.dot_general(
            all_ref[:, part],
            own_ref[...],
            (((0,), (0,)), ((), ())),
            preferred_element_type=jnp.float32,
        )
        buffer[i] = (product * scaling).astype(buffer.dtype)
        copies.append(pltpu.make_async_copy(buffer.at[i], out_hbm.at[0, part, :], sems.at[i]))
        copies[-1].start()
    for copy in copies:
        copy.wait()


def gram(place, blocks, col_width, scaling):
    count = len(blocks)
    own, width = blocks[0].shape
    height = 256
    steps = width // height
    return pl.pallas_call(
        functools.partial(gram_kernel, count, scaling),
        out_shape=jax.ShapeDtypeStruct((1, width, col_width), jnp.bfloat16),
        in_specs=[SMEM] + [VMEM] * count,
        out_specs=HBM,
        scratch_shapes=[
            pltpu.VMEM((count * own, width), jnp.bfloat16),
            pltpu.VMEM((count * own, col_width), jnp.bfloat16),
            pltpu.VMEM((steps, height, col_width), jnp.bfloat16),
            pltpu.SemaphoreType.DMA((steps,)),
        ],
        compiler_params=pltpu.CompilerParams(vmem_limit_bytes=32 * MIB),
        cost_estimate=pl.CostEstimate(
            flops=2 * count * own * width * col_width,
            bytes_accessed=width * col_width * 2 + 2 * count * own * width,
            transcendentals=0,
        ),
    )(place, *blocks)


def local(tokens, expert_ids, router_weight, window_ids, gate_weight, up_weight, down_weight):
    tok_count, feat_width = tokens.shape
    owner_count = lax.axis_size("exp")
    shard_count = lax.axis_size("dp")
    exp_place = lax.axis_index("exp").astype(jnp.int32)[None]
    dp_place = lax.axis_index("dp").astype(jnp.int32)[None]
    pieces, weighted = pack(exp_place, window_ids, expert_ids, router_weight, tokens)
    half = owner_count // 2
    pieces = [swap(piece, "exp", k) if k else piece for k, piece in enumerate(pieces)]
    bits = bits_of("dp")
    own = [jnp.concatenate(pieces[:half], axis=0), jnp.concatenate(pieces[half:], axis=0)]

    weights = load((gate_weight, up_weight, down_weight), own[1])

    def first(own, gates):
        held = {0: own}
        for bit in reversed(bits):
            held[bit] = swap(after(own, *gates.get(bit, ())), "dp", bit)
        return held

    def later(held):
        for r in range(shard_count):
            if r not in held:
                low = r & -r
                held[r] = swap(held[r ^ low], "dp", low)
        return [held[r] for r in range(shard_count)]

    a = first(own[0], {})
    b = first(own[1], {bits[-1]: [a[bit] for bit in bits], bits[0]: [a[bit] for bit in bits]})
    a[bits[-1]] = after(a[bits[-1]], weights[0])
    rows_a = later(a)
    terms_a = expert(rows_a, *weights, None)
    rows_b = later(b)
    terms_b = expert(rows_b, *weights, terms_a[0])
    out_a = reduce_blocks(terms_a, "dp").astype(jnp.bfloat16)
    a = first(out_a, {})
    out_b = reduce_blocks(terms_b, "dp").astype(jnp.bfloat16)
    out_b = after(out_b, a[bits[0]])
    rows_a = later(a)
    b = first(out_b, {})
    returned = []
    for k in range(owner_count):
        source = (out_a, out_b)[k // half]
        piece = source[(k % half) * CAP : (k % half + 1) * CAP]
        returned.append(swap(piece, "exp", k) if k else piece)
    b[bits[-1]] = after(b[bits[-1]], returned[half])
    rows_b = later(b)
    gram_rows = rows_a + rows_b
    scaling = EXPERTS_ALL / (TOPK * tok_count * owner_count * shard_count)
    gram_out = gram(dp_place, gram_rows, feat_width // shard_count, scaling)
    combined = combine(returned, weighted)
    return (combined, gram_out)


def solution(mesh):
    in_specs = (
        P(("grp", "exp", "dp"), None),
        P(("grp", "exp", "dp"), None),
        P(("grp", "exp", "dp"), None),
        P("grp"),
        P(("grp", "exp"), None, "dp"),
        P(("grp", "exp"), None, "dp"),
        P(("grp", "exp"), "dp", None),
    )
    out_specs = (P(("grp", "exp", "dp"), None), P(("grp", "exp"), None, "dp"))
    return jax.shard_map(local, mesh=mesh, in_specs=in_specs, out_specs=out_specs, check_vma=False)
```

```python
import functools

import jax
import jax.numpy as jnp
from jax import lax
from jax.experimental import pallas as pl
from jax.experimental.pallas import tpu as pltpu
from jax.sharding import PartitionSpec as P

EXPERTS_ALL = 128
TOPK = 8
CAP = 8
MIB = 1 << 20
VMEM = pl.BlockSpec(memory_space=pltpu.VMEM)
SMEM = pl.BlockSpec(memory_space=pltpu.SMEM)
HBM = pl.BlockSpec(memory_space=pltpu.HBM)


def in_hbm(x):
    return pltpu.with_memory_space_constraint(x, pltpu.HBM)


def swap(x, axis, k):
    n = lax.axis_size(axis)
    return lax.ppermute(x, axis, [(i, i ^ k) for i in range(n)])


def after(x, *others):
    return lax.optimization_barrier((x, *others))[0] if others else x


def bits_of(axis):
    n = lax.axis_size(axis)
    return [1 << i for i in range(n.bit_length() - 1)]


def reduce_blocks(blocks, axis):
    held = dict(enumerate(blocks))
    for bit in bits_of(axis):
        keep = [r for r in held if not r & bit]
        keep.sort(reverse=True)
        held = {
            r: held[r].astype(jnp.float32)
            + swap(held[r ^ bit].astype(jnp.bfloat16), axis, bit).astype(jnp.float32)
            for r in keep
        }
    return held[0]


def pack_kernel(count, place_ref, window_hbm, ids_hbm, weight_hbm, tokens_hbm, *refs):
    pieces, weighted_ref = refs[:count], refs[count]
    window_ref, ids_ref, weight_ref, tokens_ref, sems = refs[count + 1 :]
    tok_count, width = tokens_ref.shape
    step = 1024
    small = [
        pltpu.make_async_copy(source, target, sems.at[i])
        for i, (source, target) in enumerate(
            ((window_hbm, window_ref), (ids_hbm, ids_ref), (weight_hbm, weight_ref))
        )
    ]
    parts = [slice(start, start + step) for start in range(0, width, step)]
    large = [
        pltpu.make_async_copy(tokens_hbm.at[:, part], tokens_ref.at[:, part], sems.at[3 + i])
        for i, part in enumerate(parts)
    ]
    for copy in small + large:
        copy.start()
    for copy in small:
        copy.wait()
    ids = ids_ref[...]
    weights = weight_ref[...]
    routed, shares = [], []
    for k in range(count):
        match = ids == window_ref[place_ref[0] ^ k]
        routed.append(jnp.max(match.astype(jnp.float32), axis=0, keepdims=True))
        shares.append(jnp.sum(jnp.where(match, weights, 0.0), axis=0, keepdims=True))
    earlier = lax.broadcasted_iota(jnp.int32, (tok_count, tok_count), 0) < lax.broadcasted_iota(
        jnp.int32, (tok_count, tok_count), 1
    )
    ranks = jnp.dot(
        jnp.concatenate(routed, axis=0).astype(jnp.bfloat16),
        earlier.astype(jnp.bfloat16),
        preferred_element_type=jnp.float32,
    )
    slot = lax.broadcasted_iota(jnp.int32, (CAP, tok_count), 0).astype(jnp.float32)
    placing = [
        jnp.where(slot == ranks[k : k + 1], jnp.broadcast_to(routed[k], slot.shape), 0.0)
        for k in range(count)
    ]
    weighted = jnp.concatenate([placing[k] * shares[k] for k in range(count)], axis=0)
    high = weighted.astype(jnp.bfloat16)
    rest = weighted - high.astype(jnp.float32)
    middle = rest.astype(jnp.bfloat16)
    low = (rest - middle.astype(jnp.float32)).astype(jnp.bfloat16)
    weighted_ref[...] = jnp.concatenate([high, middle, low], axis=0)
    placed = jnp.concatenate(placing, axis=0).astype(jnp.bfloat16)
    for copy, part in zip(large, parts):
        copy.wait()
        rows = jnp.dot(
            placed, tokens_ref[:, part], preferred_element_type=jnp.float32
        ).astype(jnp.bfloat16)
        for k in range(count):
            pieces[k][:, part] = rows[k * CAP : (k + 1) * CAP]


def pack(place, window_ids, expert_ids, router_weight, tokens):
    count = window_ids.shape[0]
    tok_count, width = tokens.shape
    outs = pl.pallas_call(
        functools.partial(pack_kernel, count),
        out_shape=[jax.ShapeDtypeStruct((CAP, width), jnp.bfloat16)] * count
        + [jax.ShapeDtypeStruct((3 * count * CAP, tok_count), jnp.bfloat16)],
        in_specs=[SMEM] + [HBM] * 4,
        out_specs=[VMEM] * (count + 1),
        scratch_shapes=[
            pltpu.SMEM(window_ids.shape, window_ids.dtype),
            pltpu.VMEM(expert_ids.shape[::-1], expert_ids.dtype),
            pltpu.VMEM(router_weight.shape[::-1], router_weight.dtype),
            pltpu.VMEM(tokens.shape, tokens.dtype),
            pltpu.SemaphoreType.DMA((3 + width // 1024,)),
        ],
        compiler_params=pltpu.CompilerParams(vmem_limit_bytes=8 * MIB),
        cost_estimate=pl.CostEstimate(
            flops=2 * count * CAP * tok_count * width,
            bytes_accessed=2 * tok_count * width * 2,
            transcendentals=0,
        ),
    )(place, *[in_hbm(x) for x in (window_ids, expert_ids.T, router_weight.T, tokens)])
    return outs[:count], outs[count]


def load_kernel(count, *refs):
    sources, targets, sems = refs[:count], refs[-count - 1 : -1], refs[-1]
    copies = [
        pltpu.make_async_copy(source, target, sems.at[i])
        for i, (source, target) in enumerate(zip(sources, targets))
    ]
    for copy in copies:
        copy.start()
    for copy in copies:
        copy.wait()


def load(arrays, after):
    count = len(arrays)
    return pl.pallas_call(
        functools.partial(load_kernel, count),
        out_shape=[jax.ShapeDtypeStruct(x.shape, x.dtype) for x in arrays],
        in_specs=[HBM] * count + [pl.BlockSpec(memory_space=pl.ANY)],
        out_specs=[VMEM] * count,
        scratch_shapes=[pltpu.SemaphoreType.DMA((count,))],
        compiler_params=pltpu.CompilerParams(vmem_limit_bytes=16 * MIB),
        cost_estimate=pl.CostEstimate(
            flops=0,
            bytes_accessed=sum(2 * x.size * x.dtype.itemsize for x in arrays),
            transcendentals=0,
        ),
    )(*[in_hbm(x) for x in arrays], after)


def expert_kernel(count, *refs):
    rows = refs[:count]
    gate_ref, up_ref, down_ref = refs[count : count + 3]
    outs = refs[-count:]
    width = gate_ref.shape[1]
    own = rows[0].shape[0]
    step = 1024
    gate = up = 0.0
    for start in range(0, width, step):
        part = slice(start, start + step)
        x = jnp.concatenate([r[:, part] for r in rows], axis=0)
        gate += jnp.dot(x, gate_ref[0, part, :], preferred_element_type=jnp.float32)
        up += jnp.dot(x, up_ref[0, part, :], preferred_element_type=jnp.float32)
    hidden = (gate / (1.0 + jnp.exp(-gate)) * up).astype(jnp.bfloat16)
    for start in range(0, width, step):
        part = slice(start, start + step)
        y = jnp.dot(hidden, down_ref[0, :, part], preferred_element_type=jnp.float32)
        for r in range(count):
            outs[r][:, part] = y[r * own : (r + 1) * own].astype(outs[r].dtype)


def expert(rows, gate_weight, up_weight, down_weight, after):
    count = len(rows)
    own, width = rows[0].shape
    hidden = gate_weight.shape[2]
    extra = [] if after is None else [after]
    return pl.pallas_call(
        functools.partial(expert_kernel, count),
        out_shape=[
            jax.ShapeDtypeStruct((own, width), jnp.bfloat16 if r & 1 else jnp.float32)
            for r in range(count)
        ],
        in_specs=[VMEM] * (count + 3) + [pl.BlockSpec(memory_space=pl.ANY)] * len(extra),
        out_specs=[VMEM] * count,
        compiler_params=pltpu.CompilerParams(vmem_limit_bytes=24 * MIB),
        cost_estimate=pl.CostEstimate(
            flops=4 * count * own * width * hidden * 3,
            bytes_accessed=3 * width * hidden * 2 + count * own * width * 6,
            transcendentals=count * own * hidden,
        ),
    )(*rows, gate_weight, up_weight, down_weight, *extra)


def combine_kernel(count, *refs):
    rows, weighted_ref = refs[:count], refs[count]
    out_hbm, buffer, sems = refs[count + 1 :]
    weighted = weighted_ref[...].T
    steps, width = buffer.shape[0], buffer.shape[2]
    copies = []
    for i in range(steps):
        part = slice(i * width, (i + 1) * width)
        x = jnp.concatenate([r[:, part] for r in rows], axis=0)
        buffer[i] = jnp.dot(
            weighted, jnp.concatenate([x, x, x], axis=0), preferred_element_type=jnp.float32
        ).astype(buffer.dtype)
        copies.append(pltpu.make_async_copy(buffer.at[i], out_hbm.at[:, part], sems.at[i]))
        copies[-1].start()
    for copy in copies:
        copy.wait()


def combine(rows, weighted):
    count = len(rows)
    width = rows[0].shape[1]
    tok_count = weighted.shape[1]
    step = 1024
    return pl.pallas_call(
        functools.partial(combine_kernel, count),
        out_shape=jax.ShapeDtypeStruct((tok_count, width), jnp.bfloat16),
        in_specs=[VMEM] * (count + 1),
        out_specs=HBM,
        scratch_shapes=[
            pltpu.VMEM((width // step, tok_count, step), jnp.bfloat16),
            pltpu.SemaphoreType.DMA((width // step,)),
        ],
        compiler_params=pltpu.CompilerParams(vmem_limit_bytes=8 * MIB),
        cost_estimate=pl.CostEstimate(
            flops=2 * weighted.shape[0] * tok_count * width,
            bytes_accessed=2 * tok_count * width * 2,
            transcendentals=0,
        ),
    )(*rows, weighted)


def gram_kernel(count, scaling, place_ref, *refs):
    blocks = refs[:count]
    out_hbm, own_ref, buffer, sems = refs[count:]
    own = blocks[0].shape[0]
    width = own_ref.shape[1]
    columns = pl.ds(pl.multiple_of(place_ref[0] * width, width), width)
    for r in range(count):
        own_ref[r * own : (r + 1) * own, :] = blocks[r][:, columns]
    steps, height = buffer.shape[:2]
    copies = []
    for i in range(steps):
        part = slice(i * height, (i + 1) * height)
        product = lax.dot_general(
            jnp.concatenate([block[:, part] for block in blocks], axis=0),
            own_ref[...],
            (((0,), (0,)), ((), ())),
            preferred_element_type=jnp.float32,
        )
        buffer[i] = (product * scaling).astype(buffer.dtype)
        copies.append(pltpu.make_async_copy(buffer.at[i], out_hbm.at[0, part, :], sems.at[i]))
        copies[-1].start()
    for copy in copies:
        copy.wait()


def gram(place, blocks, col_width, scaling):
    count = len(blocks)
    own, width = blocks[0].shape
    height = 256
    steps = width // height
    return pl.pallas_call(
        functools.partial(gram_kernel, count, scaling),
        out_shape=jax.ShapeDtypeStruct((1, width, col_width), jnp.bfloat16),
        in_specs=[SMEM] + [VMEM] * count,
        out_specs=HBM,
        scratch_shapes=[
            pltpu.VMEM((count * own, col_width), jnp.bfloat16),
            pltpu.VMEM((steps, height, col_width), jnp.bfloat16),
            pltpu.SemaphoreType.DMA((steps,)),
        ],
        compiler_params=pltpu.CompilerParams(vmem_limit_bytes=32 * MIB),
        cost_estimate=pl.CostEstimate(
            flops=2 * count * own * width * col_width,
            bytes_accessed=width * col_width * 2 + 2 * count * own * width,
            transcendentals=0,
        ),
    )(place, *blocks)


def local(tokens, expert_ids, router_weight, window_ids, gate_weight, up_weight, down_weight):
    tok_count, feat_width = tokens.shape
    owner_count = lax.axis_size("exp")
    shard_count = lax.axis_size("dp")
    exp_place = lax.axis_index("exp").astype(jnp.int32)[None]
    dp_place = lax.axis_index("dp").astype(jnp.int32)[None]
    pieces, weighted = pack(exp_place, window_ids, expert_ids, router_weight, tokens)
    half = owner_count // 2
    pieces = [swap(piece, "exp", k) if k else piece for k, piece in enumerate(pieces)]
    bits = bits_of("dp")
    own = [jnp.concatenate(pieces[:half], axis=0), jnp.concatenate(pieces[half:], axis=0)]

    weights = load((gate_weight, up_weight, down_weight), own[1])

    def first(own, gates):
        held = {0: own}
        for bit in reversed(bits):
            held[bit] = swap(after(own, *gates.get(bit, ())), "dp", bit)
        return held

    def later(held):
        for r in range(shard_count):
            if r not in held:
                low = r & -r
                held[r] = swap(held[r ^ low], "dp", low)
        return [held[r] for r in range(shard_count)]

    a = first(own[0], {})
    b = first(own[1], {bits[-1]: [a[bit] for bit in bits], bits[0]: [a[bit] for bit in bits]})
    a[bits[-1]] = after(a[bits[-1]], weights[0])
    rows_a = later(a)
    terms_a = expert(rows_a, *weights, None)
    rows_b = later(b)
    terms_b = expert(rows_b, *weights, terms_a[0])
    out_a = reduce_blocks(terms_a, "dp").astype(jnp.bfloat16)
    a = first(out_a, {})
    out_b = reduce_blocks(terms_b, "dp").astype(jnp.bfloat16)
    out_b = after(out_b, a[bits[0]])
    rows_a = later(a)
    b = first(out_b, {})
    returned = []
    for k in range(owner_count):
        source = (out_a, out_b)[k // half]
        piece = source[(k % half) * CAP : (k % half + 1) * CAP]
        returned.append(swap(piece, "exp", k) if k else piece)
    b[bits[-1]] = after(b[bits[-1]], returned[half])
    rows_b = later(b)
    gram_rows = rows_a + rows_b
    scaling = EXPERTS_ALL / (TOPK * tok_count * owner_count * shard_count)
    gram_out = gram(dp_place, gram_rows, feat_width // shard_count, scaling)
    combined = combine([after(returned[0], b[bits[-1]], rows_a[1])] + returned[1:], weighted)
    return (combined, gram_out)


def solution(mesh):
    in_specs = (
        P(("grp", "exp", "dp"), None),
        P(("grp", "exp", "dp"), None),
        P(("grp", "exp", "dp"), None),
        P("grp"),
        P(("grp", "exp"), None, "dp"),
        P(("grp", "exp"), None, "dp"),
        P(("grp", "exp"), "dp", None),
    )
    out_specs = (P(("grp", "exp", "dp"), None), P(("grp", "exp"), None, "dp"))
    return jax.shard_map(local, mesh=mesh, in_specs=in_specs, out_specs=out_specs, check_vma=False)
```
